32 devices in a mesh: half: 2 (over y), prow: 4 (over x, core), pcol: 4 (over z).
Axes of the slice: x: 2, y: 2, z: 4, core: 2. Of those that a mesh axis runs over, the one named last changes fastest.
Arguments:
- child_pivot: float32 [2, 512, 512], P('half')
- child_panel: float32 [2, 12288, 512], P('half', 'prow'), may hold values from -1 to 1
- child_update: float32 [2, 12288, 12288], P('half', 'prow', 'pcol')
- root_front: float32 [12288, 12288], P(('half', 'prow'), 'pcol')
- row_map: int32 [2, 12288], replicated, may hold values from 0 to 12287, as said below
Outputs:
- root_lower: float32 [12288, 512], P(('half', 'prow'))
- root_update: float32 [12288, 12288], P(('half', 'prow'), 'pcol')
The draws below stay inside these ranges and needn't reach their ends.
Inputs may be any that keep to these rules, and one draw needn't show every extreme that they name: Each row_map[h] is a permutation; it sends each aligned block of 256 child indices with block number a onto one aligned block of 256 root indices whose block number equals a modulo 4.
All inputs are finite; a program needn't handle non-finite values.
Results may differ from the reference program's by a relative error of at most 0.0001.
Values sent between devices are 32-bit elements; how exact they have to be, the bound alone decides.
No kernel may reach another device: no remote copies, remote signals or barrier semaphores. Data moves between devices by JAX's collectives and lax.ppermute only.
A program may use at most 320 MiB of HBM per device.

```python
import math
import jax
import jax.numpy as jnp
from jax import lax

R = 12288
TB = 256
P2 = 512
N_PROW = 4
N_PCOL = 4


def store_layout(matrix, dimension, groups):
    array_shape = matrix.shape
    blocks = array_shape[dimension] // (groups * TB)
    split_array = matrix.reshape(array_shape[:dimension] + (blocks, groups, TB) + array_shape[dimension + 1:])
    swapped = jnp.swapaxes(split_array, dimension, dimension + 1)
    return swapped.reshape(array_shape)


def finish_symmetric(entries, key_diag, off_scale, diag_base, diag_width):
    matrix_order = entries.shape[-1]
    symmetric = (entries + jnp.swapaxes(entries, -1, -2)) * 0.5 * off_scale
    diag_values = diag_base + diag_width * jax.random.uniform(key_diag, entries.shape[:-1], jnp.float32, 0.0, 1.0)
    indices = jnp.arange(matrix_order)
    on_diagonal = indices[:, None] == indices[None, :]
    return jnp.where(on_diagonal, diag_values[..., None], symmetric)


def draw_entries(key_entries, entry_shape):
    return jax.random.uniform(key_entries, entry_shape, jnp.float32, -1.0, 1.0)


def draw_child_pivot(key, part):
    key = jax.random.fold_in(key, 3)
    key_entries, key_diag = jax.random.split(key)
    entries = draw_entries(key_entries, (2, P2, P2))
    return finish_symmetric(entries, key_diag, math.sqrt(P2) / 4.0, 0.5 * P2, 0.25 * P2)


def draw_child_update(key, part):
    key = jax.random.fold_in(key, 5)
    key_entries, key_diag = jax.random.split(key)
    entries = draw_entries(key_entries, (2, R, R))
    full_matrix = finish_symmetric(entries, key_diag, 2.0 / math.sqrt(R), 2.5, 1.0)
    return store_layout(store_layout(full_matrix, 1, N_PROW), 2, N_PCOL)


def draw_root_front(key, part):
    key = jax.random.fold_in(key, 9)
    key_entries, key_diag = jax.random.split(key)
    entries = draw_entries(key_entries, (R, R))
    indices = jnp.arange(R)
    leading = indices < P2
    both_leading = leading[:, None] & leading[None, :]
    one_leading = leading[:, None] != leading[None, :]
    off_scale = jnp.where(both_leading, 1.5 / math.sqrt(P2), jnp.where(one_leading, 5.0 / math.sqrt(P2), 2.0 / math.sqrt(R)))
    diag_base = jnp.where(leading, 4.0, 1.0)
    full_matrix = finish_symmetric(entries, key_diag, off_scale, diag_base, 1.0)
    return store_layout(store_layout(full_matrix, 0, 2 * N_PROW), 1, N_PCOL)


def draw_row_map(key, part):
    key = jax.random.fold_in(key, 7)
    per_class = R // (TB * N_PROW)
    tile_count = R // TB
    key_tiles, key_rows = jax.random.split(key)
    tile_keys = jax.random.split(key_tiles, 2 * N_PROW)
    orders = jax.vmap(lambda single: jax.random.permutation(single, per_class))(tile_keys).astype(jnp.int32)
    orders = orders.reshape(2, N_PROW, per_class)
    residues = jnp.arange(N_PROW, dtype=jnp.int32)
    targets = orders * N_PROW + residues[None, :, None]
    targets = jnp.swapaxes(targets, 1, 2).reshape(2, tile_count)
    row_keys = jax.random.split(key_rows, 2 * tile_count)
    inside = jax.vmap(lambda single: jax.random.permutation(single, TB))(row_keys).astype(jnp.int32)
    inside = inside.reshape(2, tile_count, TB)
    return (targets[:, :, None] * TB + inside).reshape(2, R).astype(jnp.int32)


def levels(stream_key, extent, pieces, least, largest):
    level = 1.0
    for axis_at, parts in pieces:
        heights = jax.random.uniform(jax.random.fold_in(jax.random.fold_in(stream_key, 6), axis_at), (parts,), jnp.float32, least / len(pieces), largest / len(pieces))
        level = level * jnp.repeat(jnp.exp(heights), extent[axis_at] // parts).reshape((-1,) + (1,) * (len(extent) - 1 - axis_at))
    return level


def setup_inputs(seed: int = 0) -> dict:
    streams_of = jax.random.split(jax.random.key(seed), 6)
    child_pivot = draw_child_pivot(jax.random.fold_in(streams_of[5], 71), 0)
    child_panel = jnp.clip(jax.random.uniform(streams_of[1], (2, R, P2), jnp.float32, -1.0, 1.0) * levels(streams_of[1], (2, R, P2), ((0, 2), (1, 4)), -0.4, 0.0), -1.0, 1.0)
    child_update = draw_child_update(jax.random.fold_in(streams_of[5], 71), 0)
    root_front = draw_root_front(jax.random.fold_in(streams_of[5], 71), 0)
    row_map = draw_row_map(jax.random.fold_in(streams_of[5], 71), 0)
    return dict(child_pivot=child_pivot, child_panel=child_panel, child_update=child_update, root_front=root_front, row_map=row_map)


def unstore(matrix, dimension, groups):
    array_shape = matrix.shape
    blocks = array_shape[dimension] // (groups * TB)
    split_array = matrix.reshape(array_shape[:dimension] + (groups, blocks, TB) + array_shape[dimension + 1:])
    swapped = jnp.swapaxes(split_array, dimension, dimension + 1)
    return swapped.reshape(array_shape)

def store(matrix, dimension, groups):
    array_shape = matrix.shape
    blocks = array_shape[dimension] // (groups * TB)
    split_array = matrix.reshape(array_shape[:dimension] + (blocks, groups, TB) + array_shape[dimension + 1:])
    swapped = jnp.swapaxes(split_array, dimension, dimension + 1)
    return swapped.reshape(array_shape)

def reference(child_pivot, child_panel, child_update, root_front, row_map):
    highest = lax.Precision.HIGHEST
    assembled = unstore(unstore(root_front, 0, 2 * N_PROW), 1, N_PCOL)
    for child_index in range(2):
        pivot_factor = jnp.linalg.cholesky(child_pivot[child_index])
        panel_rows = lax.linalg.triangular_solve(pivot_factor, unstore(child_panel[child_index], 0, N_PROW), left_side=False, lower=True, transpose_a=True)
        update_block = unstore(unstore(child_update[child_index], 0, N_PROW), 1, N_PCOL)
        contribution = update_block - jnp.dot(panel_rows, panel_rows.T, precision=highest)
        inverse = jnp.zeros((R,), jnp.int32).at[row_map[child_index]].set(jnp.arange(R, dtype=jnp.int32))
        assembled = assembled + jnp.take(jnp.take(contribution, inverse, axis=0), inverse, axis=1)
    root_factor = jnp.linalg.cholesky(assembled[:P2, :P2])
    below_rows = lax.linalg.triangular_solve(root_factor, assembled[P2:, :P2], left_side=False, lower=True, transpose_a=True)
    root_lower = jnp.concatenate([root_factor, below_rows], axis=0)
    trailing = assembled[P2:, P2:] - jnp.dot(below_rows, below_rows.T, precision=highest)
    root_update = assembled.at[P2:, P2:].set(trailing)
    return (store(root_lower, 0, 2 * N_PROW), store(store(root_update, 0, 2 * N_PROW), 1, N_PCOL))
```

```python
import functools

import jax
import jax.numpy as jnp
from jax import lax
from jax.experimental import pallas as pl
from jax.experimental.pallas import tpu as pltpu
from jax.sharding import PartitionSpec as P

TB = 256
P2 = 512
EB = 128

NN = ((1,), (0,))
NT = ((1,), (1,))
VMEM_LIMIT = 56 << 20
HEAVY = 10**12


def full_dot(left, right, dims):
    return lax.dot_general(
        left,
        right,
        (dims, ((), ())),
        precision=lax.Precision.HIGHEST,
        preferred_element_type=jnp.float32,
    )


def bf_dot(left, right, dims):
    return lax.dot_general(
        left, right, (dims, ((), ())), preferred_element_type=jnp.float32
    )


def halves(value):
    high = value.astype(jnp.bfloat16)
    low = (value - high.astype(jnp.float32)).astype(jnp.bfloat16)
    return high, low


def tripled(value):
    high, low = halves(value)
    return jnp.concatenate([high, high, low], axis=1)


def store_paired(ref, value):
    high, low = halves(value)
    depth = value.shape[1]
    ref[:, :depth] = high
    ref[:, depth : 2 * depth] = low
    ref[:, 2 * depth :] = high


def params():
    return pltpu.CompilerParams(vmem_limit_bytes=VMEM_LIMIT)


def cost(flops=0, nbytes=0):
    return pl.CostEstimate(flops=flops, bytes_accessed=nbytes, transcendentals=0)


def behind(after):
    return [pl.BlockSpec(memory_space=pl.ANY)] * len(after)


def eliminate(block):
    row_id = lax.broadcasted_iota(jnp.int32, (EB, EB), 0)
    col_id = lax.broadcasted_iota(jnp.int32, (EB, EB), 1)
    rest = block
    aside = jnp.where(row_id == col_id, 1.0, 0.0).astype(jnp.float32)
    upper_rows = []
    inverse_rows = []
    for start in range(0, EB, 8):
        count = EB - start
        columns = [
            jnp.broadcast_to(rest[:, start + k : start + k + 1], (count, EB))
            for k in range(8)
        ]
        rows = [rest[k : k + 1, :] for k in range(8)]
        aside_rows = [aside[k : k + 1, :] for k in range(8)]
        row_index = lax.broadcasted_iota(jnp.int32, (count, EB), 0)
        for k in range(8):
            scale = 1.0 / columns[k][k : k + 1, :]
            row = rows[k] * scale
            aside_row = aside_rows[k] * scale
            for later in range(k + 1, 8):
                head = columns[k][later : later + 1, :]
                rows[later] = rows[later] - head * row
                aside_rows[later] = aside_rows[later] - head * aside_row
                columns[later] = columns[later] - columns[k] * (head * scale)
            below = jnp.where(row_index > k, columns[k], 0.0)
            rest = rest - below * row
            aside = aside - below * aside_row
        upper_rows.append(rest[:8])
        inverse_rows.append(aside[:8])
        rest = rest[8:]
        aside = aside[8:]
    upper = jnp.where(col_id >= row_id, jnp.concatenate(upper_rows, axis=0), 0.0)
    pivots = jnp.sum(jnp.where(row_id == col_id, upper, 0.0), axis=1, keepdims=True)
    scale = lax.rsqrt(pivots)
    return upper * scale, jnp.concatenate(inverse_rows, axis=0) * scale


def factor_kernel(source, factor, inverse):
    count = source.shape[0] // EB
    factor[...] = jnp.zeros_like(factor)
    inverse[...] = jnp.zeros_like(inverse)

    def at(i, j):
        return (slice(i * EB, (i + 1) * EB), slice(j * EB, (j + 1) * EB))

    for i in range(count):
        for j in range(i + 1):
            factor[at(i, j)] = 0.5 * (source[at(i, j)] + source[at(j, i)].T)
    for k in range(count):
        upper, block_inverse = eliminate(factor[at(k, k)])
        factor[at(k, k)] = upper.T
        inverse[at(k, k)] = block_inverse
        for i in range(k + 1, count):
            factor[at(i, k)] = full_dot(factor[at(i, k)], block_inverse, NT)
        for i in range(k + 1, count):
            for j in range(k + 1, i + 1):
                factor[at(i, j)] = factor[at(i, j)] - full_dot(
                    factor[at(i, k)], factor[at(j, k)], NT
                )
        if k:
            done = slice(0, k * EB)
            here = slice(k * EB, (k + 1) * EB)
            left = full_dot(factor[here, done], inverse[done, done], NN)
            inverse[here, done] = -full_dot(block_inverse, left, NN)


def factor_and_inverse(matrix):
    shape = jax.ShapeDtypeStruct(matrix.shape, jnp.float32)
    return pl.pallas_call(
        factor_kernel,
        out_shape=(shape, shape),
        compiler_params=params(),
        cost_estimate=cost(),
        name="factor",
    )(matrix)


def one_hot(within, block):
    place = within[pl.ds(block, 1), :]
    target = lax.broadcasted_iota(jnp.int32, (TB, TB), 0)
    return jnp.where(target == place, 1.0, 0.0).astype(jnp.bfloat16)


def solve_placed_kernel(first, parts, tiles, blocks, within, *refs):
    sources = refs[:parts]
    inverse = refs[parts]
    out, paired = refs[-2:]
    step = pl.program_id(0)

    @pl.when(step == 0)
    def _():
        store_paired(paired, inverse[...])

    rows = sources[0][...]
    for source in sources[1:]:
        rows = rows + source[...]
    high, low = halves(bf_dot(tripled(rows), paired[...], NT))
    place = one_hot(within, blocks[first + step])
    out[...] = bf_dot(place, high, NN) + bf_dot(place, low, NN)


def solve_placed(tables, within, parts, inverse, first, count, picked, after=()):
    tiles, blocks = tables

    def source_tile(i, tiles, blocks):
        return (i, 0) if picked else (tiles[first + i], 0)

    return pl.pallas_call(
        functools.partial(solve_placed_kernel, first, len(parts)),
        out_shape=jax.ShapeDtypeStruct((count * TB, P2), jnp.float32),
        grid_spec=pltpu.PrefetchScalarGridSpec(
            num_scalar_prefetch=2,
            grid=(count,),
            in_specs=[pl.BlockSpec(within.shape, lambda i, *t: (0, 0))]
            + [pl.BlockSpec((TB, P2), source_tile)] * len(parts)
            + [pl.BlockSpec((P2, P2), lambda i, *t: (0, 0))]
            + behind(after),
            out_specs=pl.BlockSpec((TB, P2), lambda i, *t: (i, 0)),
            scratch_shapes=[pltpu.VMEM((P2, 3 * P2), jnp.bfloat16)],
        ),
        compiler_params=params(),
        cost_estimate=cost(),
        name="solve_placed",
    )(tiles, blocks, within, *parts, inverse, *after)


def solve_kernel(source, inverse, *refs):
    out, paired = refs[-2:]

    @pl.when(pl.program_id(0) == 0)
    def _():
        store_paired(paired, inverse[...])

    out[...] = bf_dot(tripled(source[...]), paired[...], NT)


def solve(rows, inverse, block, place, count, after=()):
    return pl.pallas_call(
        solve_kernel,
        out_shape=jax.ShapeDtypeStruct((count * block, P2), jnp.float32),
        grid=(count,),
        in_specs=[
            pl.BlockSpec((None,) * (rows.ndim - 2) + (block, P2), place),
            pl.BlockSpec((P2, P2), lambda i: (0, 0)),
        ]
        + behind(after),
        out_specs=pl.BlockSpec((block, P2), lambda i: (i, 0)),
        scratch_shapes=[pltpu.VMEM((P2, 3 * P2), jnp.bfloat16)],
        compiler_params=params(),
        cost_estimate=cost(),
        name="solve",
    )(rows, inverse, *after)


def pick_kernel(keep, tiles, source, *refs):
    refs[-1][...] = jnp.where(keep[0] > 0, source[...], 0.0)


def pick(keep, tiles, panel, first, count, after=()):
    return pl.pallas_call(
        pick_kernel,
        out_shape=jax.ShapeDtypeStruct((count * TB, P2), jnp.float32),
        grid_spec=pltpu.PrefetchScalarGridSpec(
            num_scalar_prefetch=2,
            grid=(count,),
            in_specs=[pl.BlockSpec((TB, P2), lambda j, keep, tiles: (tiles[first + j], 0))]
            + behind(after),
            out_specs=pl.BlockSpec((TB, P2), lambda j, *t: (j, 0)),
        ),
        compiler_params=params(),
        cost_estimate=cost(),
        name="pick",
    )(keep, tiles, panel, *after)


def contribution_kernel(rsub, count, with_base, first, *refs):
    row_blocks, col_blocks, _, _, within = refs[:5]
    refs = refs[5:]
    updates = refs[: rsub * count]
    left = refs[rsub * count]
    rights = refs[rsub * count + 1 : rsub * count + 1 + count]
    base = refs[rsub * count + 1 + count] if with_base else None
    out, paired, col_place, parts, placed = refs[-5:]
    step = pl.program_id(0)

    @pl.when(step == 0)
    def _():
        for j in range(count):
            store_paired(paired.at[j], rights[j][...])
            col_place[j] = one_hot(within, col_blocks[first + j])

    for sub in range(rsub):
        rows = slice(sub * TB, (sub + 1) * TB)
        left_parts = tripled(left[rows])
        row_place = one_hot(within, row_blocks[step * rsub + sub])
        row_place = jnp.concatenate([row_place, row_place], axis=1)
        for j in range(count):
            high, low = halves(updates[sub * count + j][...])
            parts[sub, j, :TB] = high
            parts[sub, j, TB:] = low
        for j in range(count):
            moved = bf_dot(parts[sub, j], col_place[j], NT)
            placed[sub, j] = moved.astype(jnp.bfloat16)
        for j in range(count):
            cols = slice(j * TB, (j + 1) * TB)
            tile = bf_dot(row_place, placed[sub, j], NN) - bf_dot(left_parts, paired[j], NT)
            if with_base:
                tile = tile + base[rows, cols]
            out[rows, cols] = tile


def contribution(tables, within, update, left, rights, first, count, base=None, after=(), flops=0):
    total = tables[0].shape[0]
    rsub = 2 if total % 2 == 0 and count <= 2 else 1
    in_specs = [pl.BlockSpec(within.shape, lambda i, *t: (0, 0))]
    for sub in range(rsub):
        for j in range(first, first + count):
            in_specs.append(
                pl.BlockSpec(
                    (None, TB, TB),
                    lambda i, rb, cb, rt, ct, sub=sub, j=j: (0, rt[i * rsub + sub], ct[j]),
                )
            )
    in_specs.append(pl.BlockSpec((rsub * TB, P2), lambda i, *t: (i, 0)))
    for _, tile in rights[first : first + count]:
        in_specs.append(pl.BlockSpec((TB, P2), lambda i, *t, tile=tile: (tile, 0)))
    operands = [within] + [update] * (rsub * count) + [left]
    operands += [array for array, _ in rights[first : first + count]]
    if base is not None:
        in_specs.append(
            pl.BlockSpec((rsub * TB, count * TB), lambda i, *t: (i, first // count))
        )
        operands.append(base)
    return pl.pallas_call(
        functools.partial(contribution_kernel, rsub, count, base is not None, first),
        out_shape=jax.ShapeDtypeStruct((total * TB, count * TB), jnp.float32),
        grid_spec=pltpu.PrefetchScalarGridSpec(
            num_scalar_prefetch=4,
            grid=(total // rsub,),
            in_specs=in_specs + behind(after),
            out_specs=pl.BlockSpec((rsub * TB, count * TB), lambda i, *t: (i, 0)),
            scratch_shapes=[
                pltpu.VMEM((count, TB, 3 * P2), jnp.bfloat16),
                pltpu.VMEM((count, TB, TB), jnp.bfloat16),
                pltpu.VMEM((rsub, count, 2 * TB, TB), jnp.bfloat16),
                pltpu.VMEM((rsub, count, 2 * TB, TB), jnp.bfloat16),
            ],
        ),
        compiler_params=params(),
        cost_estimate=cost(flops),
        name="contribution",
    )(*tables, *operands, *after)


def join_kernel(place, first, second, first_lead, second_lead, *refs):
    joined, shared = refs[-2:]
    rows = first.shape[0]
    for part, lead, cols in (
        (first, first_lead, slice(0, TB)),
        (second, second_lead, slice(TB, P2)),
    ):
        joined[:, cols] = part[...]
        shared[:rows, cols] = jnp.where(place[0] > 0, part[...], 0.0)
        shared[rows:, cols] = jnp.zeros((shared.shape[0] - rows, TB), jnp.float32)
    count = shared.shape[0] - rows
    here = pl.program_id(0) * count - place[1] * TB

    @pl.when((place[1] < 2) & (here >= 0) & (here < TB))
    def _():
        at = pl.ds(pl.multiple_of(here, count), count)
        shared[rows:, :TB] = first_lead[at, :]
        shared[rows:, TB:] = second_lead[at, :]


def join(place, gathered, rows, shares, after):
    share = rows // shares
    extra = P2 // shares
    return pl.pallas_call(
        join_kernel,
        out_shape=(
            jax.ShapeDtypeStruct((rows, P2), jnp.float32),
            jax.ShapeDtypeStruct((shares * (share + extra), P2), jnp.float32),
        ),
        grid_spec=pltpu.PrefetchScalarGridSpec(
            num_scalar_prefetch=1,
            grid=(shares,),
            in_specs=[
                pl.BlockSpec((share, TB), lambda i, *t: (i, 0)),
                pl.BlockSpec((share, TB), lambda i, *t: (shares + i, 0)),
                pl.BlockSpec((TB, TB), lambda i, *t: (0, 0)),
                pl.BlockSpec((TB, TB), lambda i, *t: (rows // TB, 0)),
            ]
            + behind(after),
            out_specs=(
                pl.BlockSpec((share, P2), lambda i, *t: (i, 0)),
                pl.BlockSpec((share + extra, P2), lambda i, *t: (i, 0)),
            ),
        ),
        compiler_params=params(),
        cost_estimate=cost(HEAVY),
        name="join",
    )(place, gathered, gathered, gathered, gathered, *after)


def hold_kernel(parts, *refs):
    total = refs[0][...]
    for part in refs[1:parts]:
        total = total + part[...]
    refs[-1][...] = total


def hold(values, after):
    value = values[0]
    block = value.shape[0] // 2
    spec = pl.BlockSpec((block, value.shape[1]), lambda i: (i, 0))
    return pl.pallas_call(
        functools.partial(hold_kernel, len(values)),
        out_shape=jax.ShapeDtypeStruct(value.shape, value.dtype),
        grid=(2,),
        in_specs=[spec] * len(values) + behind(after),
        out_specs=spec,
        compiler_params=params(),
        cost_estimate=cost(HEAVY),
        name="hold",
    )(*values, *after)


def finish_kernel(rsub, count, first, col_step, place, acc, incoming, left, *refs):
    rights = refs[:count]
    out, paired = refs[count:]
    step = pl.program_id(0)

    @pl.when(step == 0)
    def _():
        for j in range(count):
            store_paired(paired.at[j], rights[j][...])

    for sub in range(rsub):
        rows = slice(sub * TB, (sub + 1) * TB)
        left_parts = tripled(left[rows])
        row_block = (step * rsub + sub) * place[1] + place[0]
        for j in range(count):
            cols = slice(j * TB, (j + 1) * TB)
            product = bf_dot(left_parts, paired[j], NT)
            trailing = (row_block >= P2 // TB) & ((first + j) * col_step + place[2] >= P2 // TB)
            product = jnp.where(trailing, product, 0.0)
            out[rows, cols] = acc[rows, cols] + incoming[rows, cols] - product


def finish(place, acc, incoming, left, right, first, count, col_step):
    tiles = acc.shape[0] // TB
    rsub = 2 if tiles % 2 == 0 else 1
    in_specs = [
        pl.BlockSpec((rsub * TB, count * TB), lambda i, *t: (i, first // count)),
        pl.BlockSpec((rsub * TB, count * TB), lambda i, *t: (i, 0)),
        pl.BlockSpec((rsub * TB, P2), lambda i, *t: (i, 0)),
    ]
    for j in range(first, first + count):
        in_specs.append(
            pl.BlockSpec((TB, P2), lambda i, *t, j=j: (j % 2 * tiles + j // 2, 0))
        )
    return pl.pallas_call(
        functools.partial(finish_kernel, rsub, count, first, col_step),
        out_shape=jax.ShapeDtypeStruct(acc.shape, jnp.float32),
        grid_spec=pltpu.PrefetchScalarGridSpec(
            num_scalar_prefetch=1,
            grid=(tiles // rsub,),
            in_specs=in_specs,
            out_specs=pl.BlockSpec((rsub * TB, count * TB), lambda i, *t: (i, first // count)),
            scratch_shapes=[pltpu.VMEM((count, TB, 3 * P2), jnp.bfloat16)],
        ),
        input_output_aliases={1: 0},
        compiler_params=params(),
        cost_estimate=cost(),
        name="finish",
    )(place, acc, incoming, left, *([right] * count))


def chunks_of(tiles):
    pieces = []
    at = 0
    while at < tiles:
        count = 2 if at >= tiles // 2 and at % 2 == 0 and at + 2 < tiles else 1
        pieces.append((at, count))
        at += count
    return pieces


def local(child_pivot, child_panel, child_update, root_front, row_map):
    half_index = lax.axis_index("half")
    row_index = lax.axis_index("prow")
    col_index = lax.axis_index("pcol")
    prow_count = lax.axis_size("prow")
    pcol_count = lax.axis_size("pcol")
    col_tiles = child_update.shape[2] // TB
    root_tiles = root_front.shape[0] // TB
    half_rows = root_front.shape[0]
    panel = child_panel[0]
    chunks = chunks_of(col_tiles)

    own_map = lax.dynamic_index_in_dim(row_map, half_index, 0, keepdims=False)
    own_map = own_map.reshape(-1, TB)
    within = own_map & (TB - 1)
    target = own_map[:, 0] // TB
    tile = jnp.arange(root_tiles, dtype=jnp.int32)
    wanted = jnp.concatenate(
        [
            (tile * 2 + 1 - half_index) * prow_count + row_index,
            (tile * 2 + half_index) * prow_count + row_index,
            jnp.arange(col_tiles, dtype=jnp.int32) * pcol_count + col_index,
        ]
    )
    child_block = jnp.sum(
        jnp.where(
            wanted[:, None] == target[None, :],
            jnp.arange(target.shape[0], dtype=jnp.int32)[None, :],
            0,
        ),
        axis=1,
    )
    out_rows = child_block[:root_tiles]
    kept_rows = child_block[root_tiles : 2 * root_tiles]
    col_blocks = child_block[2 * root_tiles :]
    out_tile = out_rows // prow_count
    kept_tile = kept_rows // prow_count
    col_tile = col_blocks // pcol_count
    out_tables = (out_rows, col_blocks, out_tile, col_tile)
    kept_tables = (kept_rows, col_blocks, kept_tile, col_tile)

    keep = (row_index == col_index).astype(jnp.int32)[None]

    def fetch(first, count, after=()):
        mine = pick(keep, col_tile, panel, first, count, after)
        parts = [mine]
        for step in range(1, prow_count):
            pairs = [
                (c * pcol_count + c, (c + step) % prow_count * pcol_count + c)
                for c in range(min(prow_count, pcol_count))
            ]
            parts.append(lax.ppermute(mine, ("prow", "pcol"), pairs))
        return parts

    def solve_cols(parts, first, count):
        lower = solve_placed(
            (col_tile, col_blocks), within, parts, child_inverse, first, count, True
        )
        return [(lower, j) for j in range(count)]

    cuts = (0, 2, min(5, col_tiles - 1), col_tiles)
    spans = [(cuts[k], cuts[k + 1] - cuts[k]) for k in range(3)]
    early = fetch(*spans[0])
    _, child_inverse = factor_and_inverse(child_pivot[0])
    out_lower = solve_placed(
        (out_tile, out_rows), within, [panel], child_inverse, 0, root_tiles, False
    )
    rights = solve_cols(early, *spans[0])

    swap = [(0, 1), (1, 0)]
    incoming = []

    def send(index, after):
        outgoing = contribution(
            out_tables,
            within,
            child_update,
            out_lower,
            rights,
            *chunks[index],
            after=after,
            flops=HEAVY,
        )
        incoming.append(lax.ppermute(outgoing, "half", swap))
        return outgoing

    outgoing = send(0, [])
    outgoing = send(1, [outgoing])
    middle = fetch(*spans[1], after=[outgoing])
    kept_lower = solve_placed(
        (kept_tile, kept_rows), within, [panel], child_inverse, 0, root_tiles, False, middle[:1]
    )
    kept = contribution(
        kept_tables, within, child_update, kept_lower, rights, 0, 1, root_front
    )
    late = fetch(*spans[2], after=[kept])
    lead = hold([kept, incoming[0]], [late[0]])
    gathered = lax.all_gather(lead, "pcol", axis=0, tiled=True)
    rights += solve_cols(middle, *spans[1])
    outgoing = lead
    index = 2
    while sum(chunks[index]) <= len(rights):
        outgoing = send(index, [outgoing])
        index += 1
    row_group = (half_index * prow_count + row_index).astype(jnp.int32)
    root_panel, shared = join(
        jnp.stack([keep[0], row_group]),
        gathered,
        half_rows,
        prow_count,
        [outgoing] + incoming[1:4],
    )
    share = lax.psum_scatter(shared, "prow", scatter_dimension=0, tiled=True)
    rights += solve_cols(late, *spans[2])
    outgoing = root_panel
    stop = min(index + 2, len(chunks))
    while index < stop:
        outgoing = send(index, [outgoing])
        index += 1
    share = hold([share], [outgoing] + incoming[4:5])
    pair = lax.all_gather(share, "half", axis=0, tiled=True)
    outgoing = share
    while index < len(chunks):
        outgoing = send(index, [outgoing])
        index += 1
    pair = hold([pair], [outgoing] + incoming[5:6])
    acc = contribution(
        kept_tables,
        within,
        child_update,
        kept_lower,
        rights,
        0,
        col_tiles,
        root_front,
        [pair],
    )
    pair = lax.all_gather(pair, "prow", axis=0)
    pair = pair.reshape(prow_count, 2, -1, P2)
    rows = half_rows // prow_count
    pivots = pair[:, 0, rows:].reshape(P2, P2)
    root_factor, root_inverse = factor_and_inverse(pivots)
    block = next(b for b in (512, 256) if half_rows % b == 0)
    lower = solve(root_panel, root_inverse, block, lambda i: (i, 0), half_rows // block)
    leading = lax.dynamic_slice_in_dim(root_factor, jnp.minimum(row_group, 1) * TB, TB, 0)
    lower = lower.at[:TB].set(jnp.where(row_group < 2, leading, lower[:TB]))
    root_cols = solve(
        pair,
        root_inverse,
        rows,
        lambda i: (i % prow_count, i // prow_count, 0, 0),
        2 * prow_count,
        incoming[6:7],
    )

    place = jnp.stack(
        [row_group, jnp.asarray(2 * prow_count, jnp.int32), col_index.astype(jnp.int32)]
    )
    for (first, count), arrived in zip(chunks, incoming):
        acc = finish(place, acc, arrived, lower, root_cols, first, count, pcol_count)
    return (lower, acc)


def solution(mesh):
    placed = (
        P("half", None, None),
        P("half", "prow", None),
        P("half", "prow", "pcol"),
        P(("half", "prow"), "pcol"),
        P(),
    )
    return jax.shard_map(
        local,
        mesh=mesh,
        in_specs=placed,
        out_specs=(P(("half", "prow"), None), P(("half", "prow"), "pcol")),
        check_vma=False,
    )
```

```python
import functools

import jax
import jax.numpy as jnp
from jax import lax
from jax.experimental import pallas as pl
from jax.experimental.pallas import tpu as pltpu
from jax.sharding import PartitionSpec as P

TB = 256
P2 = 512
EB = 128

NN = ((1,), (0,))
NT = ((1,), (1,))
VMEM_LIMIT = 56 << 20
HEAVY = 10**12


def full_dot(left, right, dims):
    return lax.dot_general(
        left,
        right,
        (dims, ((), ())),
        precision=lax.Precision.HIGHEST,
        preferred_element_type=jnp.float32,
    )


def bf_dot(left, right, dims):
    return lax.dot_general(
        left, right, (dims, ((), ())), preferred_element_type=jnp.float32
    )


def halves(value):
    high = value.astype(jnp.bfloat16)
    low = (value - high.astype(jnp.float32)).astype(jnp.bfloat16)
    return high, low


def tripled(value):
    high, low = halves(value)
    return jnp.concatenate([high, high, low], axis=1)


def store_paired(ref, value):
    high, low = halves(value)
    depth = value.shape[1]
    ref[:, :depth] = high
    ref[:, depth : 2 * depth] = low
    ref[:, 2 * depth :] = high


def params():
    return pltpu.CompilerParams(vmem_limit_bytes=VMEM_LIMIT)


def cost(flops=0, nbytes=0):
    return pl.CostEstimate(flops=flops, bytes_accessed=nbytes, transcendentals=0)


def behind(after):
    return [pl.BlockSpec(memory_space=pl.ANY)] * len(after)


def eliminate(block):
    row_id = lax.broadcasted_iota(jnp.int32, (EB, EB), 0)
    col_id = lax.broadcasted_iota(jnp.int32, (EB, EB), 1)
    rest = block
    aside = jnp.where(row_id == col_id, 1.0, 0.0).astype(jnp.float32)
    upper_rows = []
    inverse_rows = []
    for start in range(0, EB, 8):
        count = EB - start
        columns = [
            jnp.broadcast_to(rest[:, start + k : start + k + 1], (count, EB))
            for k in range(8)
        ]
        rows = [rest[k : k + 1, :] for k in range(8)]
        aside_rows = [aside[k : k + 1, :] for k in range(8)]
        row_index = lax.broadcasted_iota(jnp.int32, (count, EB), 0)
        for k in range(8):
            scale = 1.0 / columns[k][k : k + 1, :]
            row = rows[k] * scale
            aside_row = aside_rows[k] * scale
            for later in range(k + 1, 8):
                head = columns[k][later : later + 1, :]
                rows[later] = rows[later] - head * row
                aside_rows[later] = aside_rows[later] - head * aside_row
                columns[later] = columns[later] - columns[k] * (head * scale)
            below = jnp.where(row_index > k, columns[k], 0.0)
            rest = rest - below * row
            aside = aside - below * aside_row
        upper_rows.append(rest[:8])
        inverse_rows.append(aside[:8])
        rest = rest[8:]
        aside = aside[8:]
    upper = jnp.where(col_id >= row_id, jnp.concatenate(upper_rows, axis=0), 0.0)
    pivots = jnp.sum(jnp.where(row_id == col_id, upper, 0.0), axis=1, keepdims=True)
    scale = lax.rsqrt(pivots)
    return upper * scale, jnp.concatenate(inverse_rows, axis=0) * scale


def factor_kernel(source, factor, inverse):
    count = source.shape[0] // EB
    factor[...] = jnp.zeros_like(factor)
    inverse[...] = jnp.zeros_like(inverse)

    def at(i, j):
        return (slice(i * EB, (i + 1) * EB), slice(j * EB, (j + 1) * EB))

    for i in range(count):
        for j in range(i + 1):
            factor[at(i, j)] = 0.5 * (source[at(i, j)] + source[at(j, i)].T)
    for k in range(count):
        upper, block_inverse = eliminate(factor[at(k, k)])
        factor[at(k, k)] = upper.T
        inverse[at(k, k)] = block_inverse
        for i in range(k + 1, count):
            factor[at(i, k)] = full_dot(factor[at(i, k)], block_inverse, NT)
        for i in range(k + 1, count):
            for j in range(k + 1, i + 1):
                factor[at(i, j)] = factor[at(i, j)] - full_dot(
                    factor[at(i, k)], factor[at(j, k)], NT
                )
        if k:
            done = slice(0, k * EB)
            here = slice(k * EB, (k + 1) * EB)
            left = full_dot(factor[here, done], inverse[done, done], NN)
            inverse[here, done] = -full_dot(block_inverse, left, NN)


def factor_and_inverse(matrix):
    shape = jax.ShapeDtypeStruct(matrix.shape, jnp.float32)
    return pl.pallas_call(
        factor_kernel,
        out_shape=(shape, shape),
        compiler_params=params(),
        cost_estimate=cost(),
        name="factor",
    )(matrix)


def one_hot(within, block):
    place = within[pl.ds(block, 1), :]
    target = lax.broadcasted_iota(jnp.int32, (TB, TB), 0)
    return jnp.where(target == place, 1.0, 0.0).astype(jnp.bfloat16)


def solve_placed_kernel(first, sub, parts, tiles, blocks, within, *refs):
    inverse = refs[sub * parts]
    out, paired = refs[-2:]
    step = pl.program_id(0)

    @pl.when(step == 0)
    def _():
        store_paired(paired, inverse[...])

    for k in range(sub):
        rows = refs[k * parts][...]
        for part in range(1, parts):
            rows = rows + refs[k * parts + part][...]
        high, low = halves(bf_dot(tripled(rows), paired[...], NT))
        place = one_hot(within, blocks[first + step * sub + k])
        out[k * TB : (k + 1) * TB] = bf_dot(place, high, NN) + bf_dot(place, low, NN)


def solve_placed(tables, within, parts, inverse, first, count, picked, after=(), skip=0):
    sub = 2 if count % 2 == 0 and skip == 0 else 1

    def source(k):
        def tile(i, tiles, blocks):
            return (i * sub + k + skip, 0) if picked else (tiles[first + i * sub + k], 0)

        return pl.BlockSpec((TB, P2), tile)

    return pl.pallas_call(
        functools.partial(solve_placed_kernel, first, sub, len(parts)),
        out_shape=jax.ShapeDtypeStruct((count * TB, P2), jnp.float32),
        grid_spec=pltpu.PrefetchScalarGridSpec(
            num_scalar_prefetch=2,
            grid=(count // sub,),
            in_specs=[pl.BlockSpec(within.shape, lambda i, *t: (0, 0))]
            + [source(k) for k in range(sub) for _ in parts]
            + [pl.BlockSpec((P2, P2), lambda i, *t: (0, 0))]
            + behind(after),
            out_specs=pl.BlockSpec((sub * TB, P2), lambda i, *t: (i, 0)),
            scratch_shapes=[pltpu.VMEM((P2, 3 * P2), jnp.bfloat16)],
        ),
        compiler_params=params(),
        cost_estimate=cost(),
        name="solve_placed",
    )(*tables, within, *(list(parts) * sub), inverse, *after)


def solve_kernel(source, inverse, out, paired):
    @pl.when(pl.program_id(0) == 0)
    def _():
        store_paired(paired, inverse[...])

    out[...] = bf_dot(tripled(source[...]), paired[...], NT)


def solve(rows, inverse, block):
    spec = pl.BlockSpec((block, P2), lambda i: (i, 0))
    return pl.pallas_call(
        solve_kernel,
        out_shape=jax.ShapeDtypeStruct(rows.shape, jnp.float32),
        grid=(rows.shape[0] // block,),
        in_specs=[spec, pl.BlockSpec((P2, P2), lambda i: (0, 0))],
        out_specs=spec,
        scratch_shapes=[pltpu.VMEM((P2, 3 * P2), jnp.bfloat16)],
        compiler_params=params(),
        cost_estimate=cost(),
        name="solve",
    )(rows, inverse)


def solve_groups(pair, inverse, rows):
    pieces = pair.shape[0]
    return pl.pallas_call(
        solve_kernel,
        out_shape=jax.ShapeDtypeStruct((2 * pieces * rows, P2), jnp.float32),
        grid=(2 * pieces,),
        in_specs=[
            pl.BlockSpec((None, None, rows, P2), lambda i: (i % pieces, i // pieces, 0, 0)),
            pl.BlockSpec((P2, P2), lambda i: (0, 0)),
        ],
        out_specs=pl.BlockSpec((rows, P2), lambda i: (i, 0)),
        scratch_shapes=[pltpu.VMEM((P2, 3 * P2), jnp.bfloat16)],
        compiler_params=params(),
        cost_estimate=cost(),
        name="solve_groups",
    )(pair, inverse)


def pick_kernel(keep, tiles, source, *refs):
    refs[-1][...] = jnp.where(keep[0] > 0, source[...], 0.0)


def pick(keep, tiles, panel, first, count, after=(), flops=0):
    return pl.pallas_call(
        pick_kernel,
        out_shape=jax.ShapeDtypeStruct((count * TB, P2), jnp.float32),
        grid_spec=pltpu.PrefetchScalarGridSpec(
            num_scalar_prefetch=2,
            grid=(count,),
            in_specs=[pl.BlockSpec((TB, P2), lambda j, keep, tiles: (tiles[first + j], 0))]
            + behind(after),
            out_specs=pl.BlockSpec((TB, P2), lambda j, *t: (j, 0)),
        ),
        compiler_params=params(),
        cost_estimate=cost(flops),
        name="pick",
    )(keep, tiles, panel, *after)


def contribution_kernel(rsub, count, with_base, first, *refs):
    row_blocks, col_blocks, _, _, within = refs[:5]
    refs = refs[5:]
    updates = refs[: rsub * count]
    left = refs[rsub * count]
    rights = refs[rsub * count + 1 : rsub * count + 1 + count]
    base = refs[rsub * count + 1 + count] if with_base else None
    out, paired, col_place, parts, placed = refs[-5:]
    step = pl.program_id(0)

    @pl.when(step == 0)
    def _():
        for j in range(count):
            store_paired(paired.at[j], rights[j][...])
            col_place[j] = one_hot(within, col_blocks[first + j])

    for sub in range(rsub):
        rows = slice(sub * TB, (sub + 1) * TB)
        left_parts = tripled(left[rows])
        row_place = one_hot(within, row_blocks[step * rsub + sub])
        row_place = jnp.concatenate([row_place, row_place], axis=1)
        for j in range(count):
            high, low = halves(updates[sub * count + j][...])
            parts[sub, j, :TB] = high
            parts[sub, j, TB:] = low
        for j in range(count):
            moved = bf_dot(parts[sub, j], col_place[j], NT)
            placed[sub, j] = moved.astype(jnp.bfloat16)
        for j in range(count):
            cols = slice(j * TB, (j + 1) * TB)
            tile = bf_dot(row_place, placed[sub, j], NN) - bf_dot(left_parts, paired[j], NT)
            if with_base:
                tile = tile + base[rows, cols]
            out[rows, cols] = tile


def contribution(tables, within, update, left, rights, first, count, base=None, after=(), flops=0):
    total = tables[0].shape[0]
    rsub = 2 if total % 2 == 0 and count <= 2 else 1
    in_specs = [pl.BlockSpec(within.shape, lambda i, *t: (0, 0))]
    for sub in range(rsub):
        for j in range(first, first + count):
            in_specs.append(
                pl.BlockSpec(
                    (None, TB, TB),
                    lambda i, rb, cb, rt, ct, sub=sub, j=j: (0, rt[i * rsub + sub], ct[j]),
                )
            )
    in_specs.append(pl.BlockSpec((rsub * TB, P2), lambda i, *t: (i, 0)))
    for _, tile in rights[first : first + count]:
        in_specs.append(pl.BlockSpec((TB, P2), lambda i, *t, tile=tile: (tile, 0)))
    operands = [within] + [update] * (rsub * count) + [left]
    operands += [array for array, _ in rights[first : first + count]]
    if base is not None:
        in_specs.append(
            pl.BlockSpec((rsub * TB, count * TB), lambda i, *t: (i, first // count))
        )
        operands.append(base)
    return pl.pallas_call(
        functools.partial(contribution_kernel, rsub, count, base is not None, first),
        out_shape=jax.ShapeDtypeStruct((total * TB, count * TB), jnp.float32),
        grid_spec=pltpu.PrefetchScalarGridSpec(
            num_scalar_prefetch=4,
            grid=(total // rsub,),
            in_specs=in_specs + behind(after),
            out_specs=pl.BlockSpec((rsub * TB, count * TB), lambda i, *t: (i, 0)),
            scratch_shapes=[
                pltpu.VMEM((count, TB, 3 * P2), jnp.bfloat16),
                pltpu.VMEM((count, TB, TB), jnp.bfloat16),
                pltpu.VMEM((rsub, count, 2 * TB, TB), jnp.bfloat16),
                pltpu.VMEM((rsub, count, 2 * TB, TB), jnp.bfloat16),
            ],
        ),
        compiler_params=params(),
        cost_estimate=cost(flops),
        name="contribution",
    )(*tables, *operands, *after)


def join_kernel(place, first, second, first_lead, second_lead, *refs):
    joined, shared = refs[-2:]
    rows = first.shape[0]
    for part, lead, cols in (
        (first, first_lead, slice(0, TB)),
        (second, second_lead, slice(TB, P2)),
    ):
        joined[:, cols] = part[...]
        shared[:rows, cols] = jnp.where(place[0] > 0, part[...], 0.0)
        shared[rows:, cols] = jnp.zeros((shared.shape[0] - rows, TB), jnp.float32)
    count = shared.shape[0] - rows
    here = pl.program_id(0) * count - place[1] * TB

    @pl.when((place[1] < 2) & (here >= 0) & (here < TB))
    def _():
        at = pl.ds(pl.multiple_of(here, count), count)
        shared[rows:, :TB] = first_lead[at, :]
        shared[rows:, TB:] = second_lead[at, :]


def join(place, gathered, rows, shares, after):
    share = rows // shares
    extra = P2 // shares
    return pl.pallas_call(
        join_kernel,
        out_shape=(
            jax.ShapeDtypeStruct((rows, P2), jnp.float32),
            jax.ShapeDtypeStruct((shares * (share + extra), P2), jnp.float32),
        ),
        grid_spec=pltpu.PrefetchScalarGridSpec(
            num_scalar_prefetch=1,
            grid=(shares,),
            in_specs=[
                pl.BlockSpec((share, TB), lambda i, *t: (i, 0)),
                pl.BlockSpec((share, TB), lambda i, *t: (shares + i, 0)),
                pl.BlockSpec((TB, TB), lambda i, *t: (0, 0)),
                pl.BlockSpec((TB, TB), lambda i, *t: (rows // TB, 0)),
            ]
            + behind(after),
            out_specs=(
                pl.BlockSpec((share, P2), lambda i, *t: (i, 0)),
                pl.BlockSpec((share + extra, P2), lambda i, *t: (i, 0)),
            ),
        ),
        compiler_params=params(),
        cost_estimate=cost(HEAVY),
        name="join",
    )(place, gathered, gathered, gathered, gathered, *after)


def hold_kernel(parts, *refs):
    total = refs[0][...]
    for part in refs[1:parts]:
        total = total + part[...]
    refs[-1][...] = total


def hold(values, after, flops=HEAVY):
    value = values[0]
    block = value.shape[0] // 2
    spec = pl.BlockSpec((block, value.shape[1]), lambda i: (i, 0))
    return pl.pallas_call(
        functools.partial(hold_kernel, len(values)),
        out_shape=jax.ShapeDtypeStruct(value.shape, value.dtype),
        grid=(2,),
        in_specs=[spec] * len(values) + behind(after),
        out_specs=spec,
        compiler_params=params(),
        cost_estimate=cost(flops),
        name="hold",
    )(*values, *after)


def finish_kernel(rsub, counts, col_step, place, acc, left, *refs):
    tiles = acc.shape[1] // TB
    incoming = refs[: len(counts)]
    rights = refs[len(counts) : len(counts) + tiles]
    out, paired = refs[-2:]
    step = pl.program_id(0)

    @pl.when(step == 0)
    def _():
        for j in range(tiles):
            store_paired(paired.at[j], rights[j][...])

    arrived = [(ref, k) for ref, count in zip(incoming, counts) for k in range(count)]
    for sub in range(rsub):
        rows = slice(sub * TB, (sub + 1) * TB)
        left_parts = tripled(left[rows])
        row_block = (step * rsub + sub) * place[1] + place[0]
        for j in range(tiles):
            cols = slice(j * TB, (j + 1) * TB)
            product = bf_dot(left_parts, paired[j], NT)
            trailing = (row_block >= P2 // TB) & (j * col_step + place[2] >= P2 // TB)
            tile = acc[rows, cols] - jnp.where(trailing, product, 0.0)
            if j < len(arrived):
                ref, k = arrived[j]
                tile = tile + ref[rows, k * TB : (k + 1) * TB]
            out[rows, cols] = tile


def finish(place, acc, incoming, left, right, col_step):
    tiles = acc.shape[0] // TB
    col_tiles = acc.shape[1] // TB
    rsub = 1
    counts = [array.shape[1] // TB for array in incoming]
    in_specs = [
        pl.BlockSpec((rsub * TB, acc.shape[1]), lambda i, *t: (i, 0)),
        pl.BlockSpec((rsub * TB, P2), lambda i, *t: (i, 0)),
    ]
    for count in counts:
        in_specs.append(pl.BlockSpec((rsub * TB, count * TB), lambda i, *t: (i, 0)))
    for j in range(col_tiles):
        in_specs.append(
            pl.BlockSpec((TB, P2), lambda i, *t, j=j: (j % 2 * tiles + j // 2, 0))
        )
    return pl.pallas_call(
        functools.partial(finish_kernel, rsub, counts, col_step),
        out_shape=jax.ShapeDtypeStruct(acc.shape, jnp.float32),
        grid_spec=pltpu.PrefetchScalarGridSpec(
            num_scalar_prefetch=1,
            grid=(tiles // rsub,),
            in_specs=in_specs,
            out_specs=pl.BlockSpec((rsub * TB, acc.shape[1]), lambda i, *t: (i, 0)),
            scratch_shapes=[pltpu.VMEM((col_tiles, TB, 3 * P2), jnp.bfloat16)],
        ),
        input_output_aliases={1: 0},
        compiler_params=params(),
        cost_estimate=cost(),
        name="finish",
    )(place, acc, left, *incoming, *([right] * col_tiles))


def add_kernel(acc, incoming, out):
    out[...] = acc[...] + incoming[...]


def add_piece(acc, incoming, first, count):
    rows = acc.shape[0]
    block = next(b for b in (768, 512, 256) if rows % b == 0)
    spec = pl.BlockSpec((block, count * TB), lambda i: (i, first // count))
    return pl.pallas_call(
        add_kernel,
        out_shape=jax.ShapeDtypeStruct(acc.shape, jnp.float32),
        grid=(rows // block,),
        in_specs=[spec, pl.BlockSpec((block, count * TB), lambda i: (i, 0))],
        out_specs=spec,
        input_output_aliases={0: 0},
        compiler_params=params(),
        cost_estimate=cost(),
        name="add_piece",
    )(acc, incoming)


def chunks_of(tiles):
    pieces = [(0, 1), (1, 2), (3, 1), (4, 1), (5, 1)]
    at = 6
    while at < tiles:
        count = 2 if at % 2 == 0 and at + 2 < tiles else 1
        pieces.append((at, count))
        at += count
    return pieces


def local(child_pivot, child_panel, child_update, root_front, row_map):
    half_index = lax.axis_index("half")
    row_index = lax.axis_index("prow")
    col_index = lax.axis_index("pcol")
    prow_count = lax.axis_size("prow")
    pcol_count = lax.axis_size("pcol")
    col_tiles = child_update.shape[2] // TB
    root_tiles = root_front.shape[0] // TB
    half_rows = root_front.shape[0]
    panel = child_panel[0]
    chunks = chunks_of(col_tiles)

    own_map = lax.dynamic_index_in_dim(row_map, half_index, 0, keepdims=False)
    own_map = own_map.reshape(-1, TB)
    within = own_map & (TB - 1)
    target = own_map[:, 0] // TB
    tile = jnp.arange(root_tiles, dtype=jnp.int32)
    wanted = jnp.concatenate(
        [
            (tile * 2 + 1 - half_index) * prow_count + row_index,
            (tile * 2 + half_index) * prow_count + row_index,
            jnp.arange(col_tiles, dtype=jnp.int32) * pcol_count + col_index,
        ]
    )
    child_block = jnp.sum(
        jnp.where(
            wanted[:, None] == target[None, :],
            jnp.arange(target.shape[0], dtype=jnp.int32)[None, :],
            0,
        ),
        axis=1,
    )
    out_rows = child_block[:root_tiles]
    kept_rows = child_block[root_tiles : 2 * root_tiles]
    col_blocks = child_block[2 * root_tiles :]
    out_tile = out_rows // prow_count
    kept_tile = kept_rows // prow_count
    col_tile = col_blocks // pcol_count
    out_tables = (out_rows, col_blocks, out_tile, col_tile)
    kept_tables = (kept_rows, col_blocks, kept_tile, col_tile)

    keep = (row_index == col_index).astype(jnp.int32)[None]

    def fetch(first, count, after):
        mine = pick(keep, col_tile, panel, first, count, after, HEAVY)
        parts = [mine]
        for step in range(1, prow_count):
            pairs = [
                (c * pcol_count + c, (c + step) % prow_count * pcol_count + c)
                for c in range(min(prow_count, pcol_count))
            ]
            parts.append(lax.ppermute(mine, ("prow", "pcol"), pairs))
        return parts

    def solve_cols(parts, first, count, after=(), skip=0):
        lower = solve_placed(
            (col_tile, col_blocks), within, parts, child_inverse, first, count, True, after, skip
        )
        return [(lower, j) for j in range(count)]

    cuts = (0, 3, min(6, col_tiles - 1), col_tiles)
    spans = [(cuts[k], cuts[k + 1] - cuts[k]) for k in range(3)]
    early = fetch(*spans[0], [])
    _, child_inverse = factor_and_inverse(child_pivot[0])
    out_lower = solve_placed(
        (out_tile, out_rows), within, [panel], child_inverse, 0, root_tiles, False
    )
    rights = solve_cols(early, 0, 1)

    swap = [(0, 1), (1, 0)]
    incoming = []

    def send(index, after):
        outgoing = contribution(
            out_tables,
            within,
            child_update,
            out_lower,
            rights,
            *chunks[index],
            after=after,
            flops=0,
        )
        incoming.append(lax.ppermute(outgoing, "half", swap))
        return outgoing

    outgoing = send(0, [])
    middle = fetch(*spans[1], [outgoing])
    rights += solve_cols(early, 1, spans[0][1] - 1, [middle[0]], 1)
    outgoing = send(1, [outgoing])
    kept_lower = solve_placed(
        (kept_tile, kept_rows), within, [panel], child_inverse, 0, root_tiles, False, [outgoing]
    )
    kept = contribution(
        kept_tables, within, child_update, kept_lower, rights, 0, 1, root_front
    )
    lead = hold([kept, incoming[0]], [])
    gathered = lax.all_gather(lead, "pcol", axis=0, tiled=True)
    rights += solve_cols(middle, *spans[1])
    late = fetch(*spans[2], [lead])
    outgoing = late[0]
    for index in (2, 3):
        outgoing = send(index, [outgoing])
    if sum(chunks[4]) <= len(rights):
        outgoing = send(4, [outgoing])
    rights += solve_cols(late, *spans[2], after=[outgoing, incoming[1]])
    if len(incoming) < 5:
        outgoing = send(4, [outgoing])
    row_group = (half_index * prow_count + row_index).astype(jnp.int32)
    root_panel, shared = join(
        jnp.stack([keep[0], row_group]),
        gathered,
        half_rows,
        prow_count,
        [rights[-1][0]] + incoming[2:4],
    )
    share = lax.psum_scatter(shared, "prow", scatter_dimension=0, tiled=True)
    outgoing = root_panel
    for index in range(5, len(chunks)):
        outgoing = send(index, [outgoing])
    share = hold([share], [outgoing] + incoming[4:5])
    rows = half_rows // prow_count
    pair = lax.all_gather(share, "half", axis=0, tiled=True)
    pair = hold([pair], incoming[5:6])
    acc = contribution(
        kept_tables,
        within,
        child_update,
        kept_lower,
        rights,
        0,
        col_tiles,
        root_front,
        [pair],
    )
    pair = lax.all_gather(pair, "prow", axis=0).reshape(prow_count, 2, -1, P2)
    pivots = pair[:, 0, rows:].reshape(P2, P2)
    root_factor, root_inverse = factor_and_inverse(pivots)
    block = next(b for b in (512, 256) if half_rows % b == 0)
    lower = solve(root_panel, root_inverse, block)
    leading = lax.dynamic_slice_in_dim(root_factor, jnp.minimum(row_group, 1) * TB, TB, 0)
    lower = lower.at[:TB].set(jnp.where(row_group < 2, leading, lower[:TB]))
    root_cols = solve_groups(pair, root_inverse, rows)

    place = jnp.stack(
        [row_group, jnp.asarray(2 * prow_count, jnp.int32), col_index.astype(jnp.int32)]
    )
    early_count = min(6, len(chunks) - 1)
    acc = finish(place, acc, incoming[:early_count], lower, root_cols, pcol_count)
    for (first, count), arrived in list(zip(chunks, incoming))[early_count:]:
        acc = add_piece(acc, arrived, first, count)
    return (lower, acc)


def solution(mesh):
    placed = (
        P("half", None, None),
        P("half", "prow", None),
        P("half", "prow", "pcol"),
        P(("half", "prow"), "pcol"),
        P(),
    )
    return jax.shard_map(
        local,
        mesh=mesh,
        in_specs=placed,
        out_specs=(P(("half", "prow"), None), P(("half", "prow"), "pcol")),
        check_vma=False,
    )
```

```python
import functools

import jax
import jax.numpy as jnp
from jax import lax
from jax.experimental import pallas as pl
from jax.experimental.pallas import tpu as pltpu
from jax.sharding import PartitionSpec as P

TB = 256
P2 = 512
EB = 128

NN = ((1,), (0,))
NT = ((1,), (1,))
VMEM_LIMIT = 56 << 20
HEAVY = 10**12


def full_dot(left, right, dims):
    return lax.dot_general(
        left,
        right,
        (dims, ((), ())),
        precision=lax.Precision.HIGHEST,
        preferred_element_type=jnp.float32,
    )


def bf_dot(left, right, dims):
    return lax.dot_general(
        left, right, (dims, ((), ())), preferred_element_type=jnp.float32
    )


def halves(value):
    high = value.astype(jnp.bfloat16)
    low = (value - high.astype(jnp.float32)).astype(jnp.bfloat16)
    return high, low


def tripled(value):
    high, low = halves(value)
    return jnp.concatenate([high, high, low], axis=1)


def store_paired(ref, value):
    high, low = halves(value)
    depth = value.shape[1]
    ref[:, :depth] = high
    ref[:, depth : 2 * depth] = low
    ref[:, 2 * depth :] = high


def params():
    return pltpu.CompilerParams(vmem_limit_bytes=VMEM_LIMIT)


def cost(flops=0, nbytes=0):
    return pl.CostEstimate(flops=flops, bytes_accessed=nbytes, transcendentals=0)


def behind(after):
    return [pl.BlockSpec(memory_space=pl.ANY)] * len(after)


def eliminate(block):
    row_id = lax.broadcasted_iota(jnp.int32, (EB, EB), 0)
    col_id = lax.broadcasted_iota(jnp.int32, (EB, EB), 1)
    rest = block
    aside = jnp.where(row_id == col_id, 1.0, 0.0).astype(jnp.float32)
    upper_rows = []
    inverse_rows = []
    for start in range(0, EB, 8):
        count = EB - start
        columns = [
            jnp.broadcast_to(rest[:, start + k : start + k + 1], (count, EB))
            for k in range(8)
        ]
        rows = [rest[k : k + 1, :] for k in range(8)]
        aside_rows = [aside[k : k + 1, :] for k in range(8)]
        row_index = lax.broadcasted_iota(jnp.int32, (count, EB), 0)
        for k in range(8):
            scale = 1.0 / columns[k][k : k + 1, :]
            row = rows[k] * scale
            aside_row = aside_rows[k] * scale
            for later in range(k + 1, 8):
                head = columns[k][later : later + 1, :]
                rows[later] = rows[later] - head * row
                aside_rows[later] = aside_rows[later] - head * aside_row
                columns[later] = columns[later] - columns[k] * (head * scale)
            below = jnp.where(row_index > k, columns[k], 0.0)
            rest = rest - below * row
            aside = aside - below * aside_row
        upper_rows.append(rest[:8])
        inverse_rows.append(aside[:8])
        rest = rest[8:]
        aside = aside[8:]
    upper = jnp.where(col_id >= row_id, jnp.concatenate(upper_rows, axis=0), 0.0)
    pivots = jnp.sum(jnp.where(row_id == col_id, upper, 0.0), axis=1, keepdims=True)
    scale = lax.rsqrt(pivots)
    return upper * scale, jnp.concatenate(inverse_rows, axis=0) * scale


def factor_kernel(source, factor, inverse):
    count = source.shape[0] // EB
    factor[...] = jnp.zeros_like(factor)
    inverse[...] = jnp.zeros_like(inverse)

    def at(i, j):
        return (slice(i * EB, (i + 1) * EB), slice(j * EB, (j + 1) * EB))

    for i in range(count):
        for j in range(i + 1):
            factor[at(i, j)] = 0.5 * (source[at(i, j)] + source[at(j, i)].T)
    for k in range(count):
        upper, block_inverse = eliminate(factor[at(k, k)])
        factor[at(k, k)] = upper.T
        inverse[at(k, k)] = block_inverse
        for i in range(k + 1, count):
            factor[at(i, k)] = full_dot(factor[at(i, k)], block_inverse, NT)
        for i in range(k + 1, count):
            for j in range(k + 1, i + 1):
                factor[at(i, j)] = factor[at(i, j)] - full_dot(
                    factor[at(i, k)], factor[at(j, k)], NT
                )
        if k:
            done = slice(0, k * EB)
            here = slice(k * EB, (k + 1) * EB)
            left = full_dot(factor[here, done], inverse[done, done], NN)
            inverse[here, done] = -full_dot(block_inverse, left, NN)


def factor_and_inverse(matrix):
    shape = jax.ShapeDtypeStruct(matrix.shape, jnp.float32)
    return pl.pallas_call(
        factor_kernel,
        out_shape=(shape, shape),
        compiler_params=params(),
        cost_estimate=cost(),
        name="factor",
    )(matrix)


def one_hot(within, block):
    place = within[pl.ds(block, 1), :]
    target = lax.broadcasted_iota(jnp.int32, (TB, TB), 0)
    return jnp.where(target == place, 1.0, 0.0).astype(jnp.bfloat16)


def solve_placed_kernel(first, sub, parts, blocks, within, *refs):
    inverse = refs[sub * parts]
    out, paired = refs[-2:]
    step = pl.program_id(0)

    @pl.when(step == 0)
    def _():
        store_paired(paired, inverse[...])

    for k in range(sub):
        rows = refs[k * parts][...]
        for part in range(1, parts):
            rows = rows + refs[k * parts + part][...]
        high, low = halves(bf_dot(tripled(rows), paired[...], NT))
        place = one_hot(within, blocks[first + step * sub + k])
        out[k * TB : (k + 1) * TB] = bf_dot(place, high, NN) + bf_dot(place, low, NN)


def solve_placed(tables, within, parts, inverse, first, count, picked, after=(), skip=0):
    blocks, begin, groups = tables
    first = begin + first
    sub = 2 if count % 2 == 0 and skip == 0 else 1

    def source(k):
        def tile(i, blocks):
            if picked:
                return (i * sub + k + skip, 0)
            return (lax.div(blocks[first + i * sub + k], jnp.int32(groups)), 0)

        return pl.BlockSpec((TB, P2), tile)

    return pl.pallas_call(
        functools.partial(solve_placed_kernel, first, sub, len(parts)),
        out_shape=jax.ShapeDtypeStruct((count * TB, P2), jnp.float32),
        grid_spec=pltpu.PrefetchScalarGridSpec(
            num_scalar_prefetch=1,
            grid=(count // sub,),
            in_specs=[pl.BlockSpec(within.shape, lambda i, *t: (0, 0))]
            + [source(k) for k in range(sub) for _ in parts]
            + [pl.BlockSpec((P2, P2), lambda i, *t: (0, 0))]
            + behind(after),
            out_specs=pl.BlockSpec((sub * TB, P2), lambda i, *t: (i, 0)),
            scratch_shapes=[pltpu.VMEM((P2, 3 * P2), jnp.bfloat16)],
        ),
        compiler_params=params(),
        cost_estimate=cost(),
        name="solve_placed",
    )(blocks, within, *(list(parts) * sub), inverse, *after)


def solve_kernel(source, inverse, out, paired):
    @pl.when(pl.program_id(0) == 0)
    def _():
        store_paired(paired, inverse[...])

    out[...] = bf_dot(tripled(source[...]), paired[...], NT)


def solve(rows, inverse, block):
    spec = pl.BlockSpec((block, P2), lambda i: (i, 0))
    return pl.pallas_call(
        solve_kernel,
        out_shape=jax.ShapeDtypeStruct(rows.shape, jnp.float32),
        grid=(rows.shape[0] // block,),
        in_specs=[spec, pl.BlockSpec((P2, P2), lambda i: (0, 0))],
        out_specs=spec,
        scratch_shapes=[pltpu.VMEM((P2, 3 * P2), jnp.bfloat16)],
        compiler_params=params(),
        cost_estimate=cost(),
        name="solve",
    )(rows, inverse)


def solve_groups(pair, inverse, rows):
    pieces = pair.shape[0]
    return pl.pallas_call(
        solve_kernel,
        out_shape=jax.ShapeDtypeStruct((2 * pieces * rows, P2), jnp.float32),
        grid=(2 * pieces,),
        in_specs=[
            pl.BlockSpec((None, None, rows, P2), lambda i: (i % pieces, i // pieces, 0, 0)),
            pl.BlockSpec((P2, P2), lambda i: (0, 0)),
        ],
        out_specs=pl.BlockSpec((rows, P2), lambda i: (i, 0)),
        scratch_shapes=[pltpu.VMEM((P2, 3 * P2), jnp.bfloat16)],
        compiler_params=params(),
        cost_estimate=cost(),
        name="solve_groups",
    )(pair, inverse)


def pick_kernel(keep, blocks, source, *refs):
    refs[-1][...] = jnp.where(keep[0] > 0, source[...], 0.0)


def pick(keep, tables, panel, first, count, after=(), flops=0):
    blocks, begin, groups = tables
    first = begin + first
    return pl.pallas_call(
        pick_kernel,
        out_shape=jax.ShapeDtypeStruct((count * TB, P2), jnp.float32),
        grid_spec=pltpu.PrefetchScalarGridSpec(
            num_scalar_prefetch=2,
            grid=(count,),
            in_specs=[
                pl.BlockSpec(
                    (TB, P2),
                    lambda j, keep, blocks: (lax.div(blocks[first + j], jnp.int32(groups)), 0),
                )
            ]
            + behind(after),
            out_specs=pl.BlockSpec((TB, P2), lambda j, *t: (j, 0)),
        ),
        compiler_params=params(),
        cost_estimate=cost(flops),
        name="pick",
    )(keep, blocks, panel, *after)


def contribution_kernel(rsub, count, with_base, row_first, col_first, blocks, within, *refs):
    updates = refs[: rsub * count]
    left = refs[rsub * count]
    rights = refs[rsub * count + 1 : rsub * count + 1 + count]
    base = refs[rsub * count + 1 + count] if with_base else None
    out, paired, col_place, parts, placed = refs[-5:]
    step = pl.program_id(0)

    @pl.when(step == 0)
    def _():
        for j in range(count):
            store_paired(paired.at[j], rights[j][...])
            col_place[j] = one_hot(within, blocks[col_first + j])

    for sub in range(rsub):
        rows = slice(sub * TB, (sub + 1) * TB)
        left_parts = tripled(left[rows])
        row_place = one_hot(within, blocks[row_first + step * rsub + sub])
        row_place = jnp.concatenate([row_place, row_place], axis=1)
        for j in range(count):
            high, low = halves(updates[sub * count + j][...])
            parts[sub, j, :TB] = high
            parts[sub, j, TB:] = low
        for j in range(count):
            moved = bf_dot(parts[sub, j], col_place[j], NT)
            placed[sub, j] = moved.astype(jnp.bfloat16)
        for j in range(count):
            cols = slice(j * TB, (j + 1) * TB)
            tile = bf_dot(row_place, placed[sub, j], NN) - bf_dot(left_parts, paired[j], NT)
            if with_base:
                tile = tile + base[rows, cols]
            out[rows, cols] = tile


def contribution(tables, within, update, left, rights, first, count, base=None, after=(), flops=0):
    blocks, row_first, total, row_groups, col_first, col_groups = tables
    col_first = col_first + first
    rsub = 2 if total % 2 == 0 and count <= 2 else 1
    in_specs = [pl.BlockSpec(within.shape, lambda i, *t: (0, 0))]
    for sub in range(rsub):
        for j in range(count):

            def place(i, blocks, sub=sub, j=j):
                row = blocks[row_first + i * rsub + sub]
                col = blocks[col_first + j]
                return (0, lax.div(row, jnp.int32(row_groups)), lax.div(col, jnp.int32(col_groups)))

            in_specs.append(pl.BlockSpec((None, TB, TB), place))
    in_specs.append(pl.BlockSpec((rsub * TB, P2), lambda i, *t: (i, 0)))
    for _, tile in rights[first : first + count]:
        in_specs.append(pl.BlockSpec((TB, P2), lambda i, *t, tile=tile: (tile, 0)))
    operands = [within] + [update] * (rsub * count) + [left]
    operands += [array for array, _ in rights[first : first + count]]
    if base is not None:
        in_specs.append(
            pl.BlockSpec((rsub * TB, count * TB), lambda i, *t: (i, first // count))
        )
        operands.append(base)
    return pl.pallas_call(
        functools.partial(
            contribution_kernel, rsub, count, base is not None, row_first, col_first
        ),
        out_shape=jax.ShapeDtypeStruct((total * TB, count * TB), jnp.float32),
        grid_spec=pltpu.PrefetchScalarGridSpec(
            num_scalar_prefetch=1,
            grid=(total // rsub,),
            in_specs=in_specs + behind(after),
            out_specs=pl.BlockSpec((rsub * TB, count * TB), lambda i, *t: (i, 0)),
            scratch_shapes=[
                pltpu.VMEM((count, TB, 3 * P2), jnp.bfloat16),
                pltpu.VMEM((count, TB, TB), jnp.bfloat16),
                pltpu.VMEM((rsub, count, 2 * TB, TB), jnp.bfloat16),
                pltpu.VMEM((rsub, count, 2 * TB, TB), jnp.bfloat16),
            ],
        ),
        compiler_params=params(),
        cost_estimate=cost(flops),
        name="contribution",
    )(blocks, *operands, *after)


def join_kernel(place, first, second, first_lead, second_lead, *refs):
    joined, shared = refs[-2:]
    rows = first.shape[0]
    for part, lead, cols in (
        (first, first_lead, slice(0, TB)),
        (second, second_lead, slice(TB, P2)),
    ):
        joined[:, cols] = part[...]
        shared[:rows, cols] = jnp.where(place[0] > 0, part[...], 0.0)
        shared[rows:, cols] = jnp.zeros((shared.shape[0] - rows, TB), jnp.float32)
    count = shared.shape[0] - rows
    here = pl.program_id(0) * count - place[1] * TB

    @pl.when((place[1] < 2) & (here >= 0) & (here < TB))
    def _():
        at = pl.ds(pl.multiple_of(here, count), count)
        shared[rows:, :TB] = first_lead[at, :]
        shared[rows:, TB:] = second_lead[at, :]


def join(place, gathered, rows, shares, after):
    share = rows // shares
    extra = P2 // shares
    return pl.pallas_call(
        join_kernel,
        out_shape=(
            jax.ShapeDtypeStruct((rows, P2), jnp.float32),
            jax.ShapeDtypeStruct((shares * (share + extra), P2), jnp.float32),
        ),
        grid_spec=pltpu.PrefetchScalarGridSpec(
            num_scalar_prefetch=1,
            grid=(shares,),
            in_specs=[
                pl.BlockSpec((share, TB), lambda i, *t: (i, 0)),
                pl.BlockSpec((share, TB), lambda i, *t: (shares + i, 0)),
                pl.BlockSpec((TB, TB), lambda i, *t: (0, 0)),
                pl.BlockSpec((TB, TB), lambda i, *t: (rows // TB, 0)),
            ]
            + behind(after),
            out_specs=(
                pl.BlockSpec((share, P2), lambda i, *t: (i, 0)),
                pl.BlockSpec((share + extra, P2), lambda i, *t: (i, 0)),
            ),
        ),
        compiler_params=params(),
        cost_estimate=cost(HEAVY),
        name="join",
    )(place, gathered, gathered, gathered, gathered, *after)


def hold_kernel(parts, *refs):
    total = refs[0][...]
    for part in refs[1:parts]:
        total = total + part[...]
    refs[-1][...] = total


def hold(values, after, flops=HEAVY):
    value = values[0]
    block = value.shape[0] // 2
    spec = pl.BlockSpec((block, value.shape[1]), lambda i: (i, 0))
    return pl.pallas_call(
        functools.partial(hold_kernel, len(values)),
        out_shape=jax.ShapeDtypeStruct(value.shape, value.dtype),
        grid=(2,),
        in_specs=[spec] * len(values) + behind(after),
        out_specs=spec,
        compiler_params=params(),
        cost_estimate=cost(flops),
        name="hold",
    )(*values, *after)


def lower_part_kernel(source, *refs):
    refs[-1][...] = source[...]


def lower_part(pair, rows, after):
    spec = pl.BlockSpec((None, rows, P2), lambda i: (i, 0, 0))
    return pl.pallas_call(
        lower_part_kernel,
        out_shape=jax.ShapeDtypeStruct((2, rows, P2), pair.dtype),
        grid=(2,),
        in_specs=[spec] + behind(after),
        out_specs=spec,
        compiler_params=params(),
        cost_estimate=cost(HEAVY),
        name="lower_part",
    )(pair, *after)


def finish_kernel(rsub, counts, col_step, place, acc, left, *refs):
    tiles = acc.shape[1] // TB
    incoming = refs[: len(counts)]
    rights = refs[len(counts) : len(counts) + tiles]
    out, paired = refs[-2:]
    step = pl.program_id(0)

    @pl.when(step == 0)
    def _():
        for j in range(tiles):
            store_paired(paired.at[j], rights[j][...])

    arrived = [(ref, k) for ref, count in zip(incoming, counts) for k in range(count)]
    for sub in range(rsub):
        rows = slice(sub * TB, (sub + 1) * TB)
        left_parts = tripled(left[rows])
        row_block = (step * rsub + sub) * place[1] + place[0]
        for j in range(tiles):
            cols = slice(j * TB, (j + 1) * TB)
            product = bf_dot(left_parts, paired[j], NT)
            trailing = (row_block >= P2 // TB) & (j * col_step + place[2] >= P2 // TB)
            tile = acc[rows, cols] - jnp.where(trailing, product, 0.0)
            if j < len(arrived):
                ref, k = arrived[j]
                tile = tile + ref[rows, k * TB : (k + 1) * TB]
            out[rows, cols] = tile


def finish(place, acc, incoming, left, right, col_step):
    tiles = acc.shape[0] // TB
    col_tiles = acc.shape[1] // TB
    rsub = 1
    counts = [array.shape[1] // TB for array in incoming]
    in_specs = [
        pl.BlockSpec((rsub * TB, acc.shape[1]), lambda i, *t: (i, 0)),
        pl.BlockSpec((rsub * TB, P2), lambda i, *t: (i, 0)),
    ]
    for count in counts:
        in_specs.append(pl.BlockSpec((rsub * TB, count * TB), lambda i, *t: (i, 0)))
    for j in range(col_tiles):
        in_specs.append(
            pl.BlockSpec((TB, P2), lambda i, *t, j=j: (j % 2 * tiles + j // 2, 0))
        )
    return pl.pallas_call(
        functools.partial(finish_kernel, rsub, counts, col_step),
        out_shape=jax.ShapeDtypeStruct(acc.shape, jnp.float32),
        grid_spec=pltpu.PrefetchScalarGridSpec(
            num_scalar_prefetch=1,
            grid=(tiles // rsub,),
            in_specs=in_specs,
            out_specs=pl.BlockSpec((rsub * TB, acc.shape[1]), lambda i, *t: (i, 0)),
            scratch_shapes=[pltpu.VMEM((col_tiles, TB, 3 * P2), jnp.bfloat16)],
        ),
        input_output_aliases={1: 0},
        compiler_params=params(),
        cost_estimate=cost(),
        name="finish",
    )(place, acc, left, *incoming, *([right] * col_tiles))


def add_kernel(acc, incoming, out):
    out[...] = acc[...] + incoming[...]


def add_piece(acc, incoming, first, count):
    rows = acc.shape[0]
    block = next(b for b in (768, 512, 256) if rows % b == 0)
    spec = pl.BlockSpec((block, count * TB), lambda i: (i, first // count))
    return pl.pallas_call(
        add_kernel,
        out_shape=jax.ShapeDtypeStruct(acc.shape, jnp.float32),
        grid=(rows // block,),
        in_specs=[spec, pl.BlockSpec((block, count * TB), lambda i: (i, 0))],
        out_specs=spec,
        input_output_aliases={0: 0},
        compiler_params=params(),
        cost_estimate=cost(),
        name="add_piece",
    )(acc, incoming)


def chunks_of(tiles):
    pieces = [(0, 1), (1, 2), (3, 1), (4, 1), (5, 1)]
    at = 6
    while at < tiles:
        count = 2 if at % 2 == 0 and at + 2 < tiles else 1
        pieces.append((at, count))
        at += count
    return pieces


def local(child_pivot, child_panel, child_update, root_front, row_map):
    half_index = lax.axis_index("half")
    row_index = lax.axis_index("prow")
    col_index = lax.axis_index("pcol")
    prow_count = lax.axis_size("prow")
    pcol_count = lax.axis_size("pcol")
    col_tiles = child_update.shape[2] // TB
    root_tiles = root_front.shape[0] // TB
    half_rows = root_front.shape[0]
    panel = child_panel[0]
    chunks = chunks_of(col_tiles)

    own_map = lax.dynamic_index_in_dim(row_map, half_index, 0, keepdims=False)
    own_map = own_map.reshape(-1, TB)
    within = own_map & (TB - 1)
    target = own_map[:, 0] // TB
    tile = jnp.arange(root_tiles, dtype=jnp.int32)
    wanted = jnp.concatenate(
        [
            (tile * 2 + 1 - half_index) * prow_count + row_index,
            (tile * 2 + half_index) * prow_count + row_index,
            jnp.arange(col_tiles, dtype=jnp.int32) * pcol_count + col_index,
        ]
    )
    child_block = jnp.sum(
        jnp.where(
            wanted[:, None] == target[None, :],
            jnp.arange(target.shape[0], dtype=jnp.int32)[None, :],
            0,
        ),
        axis=1,
    )
    col_table = (child_block, 2 * root_tiles, pcol_count)
    out_tables = (child_block, 0, root_tiles, prow_count) + col_table[1:]
    kept_tables = (child_block, root_tiles, root_tiles, prow_count) + col_table[1:]

    keep = (row_index == col_index).astype(jnp.int32)[None]

    def fetch(first, count, after):
        mine = pick(keep, col_table, panel, first, count, after, HEAVY)
        parts = [mine]
        for step in range(1, prow_count):
            pairs = [
                (c * pcol_count + c, (c + step) % prow_count * pcol_count + c)
                for c in range(min(prow_count, pcol_count))
            ]
            parts.append(lax.ppermute(mine, ("prow", "pcol"), pairs))
        return parts

    def solve_cols(parts, first, count, after=(), skip=0):
        lower = solve_placed(
            col_table, within, parts, child_inverse, first, count, True, after, skip
        )
        return [(lower, j) for j in range(count)]

    cuts = (0, 3, min(6, col_tiles - 1), col_tiles)
    spans = [(cuts[k], cuts[k + 1] - cuts[k]) for k in range(3)]
    early = fetch(*spans[0], [])
    _, child_inverse = factor_and_inverse(child_pivot[0])
    out_lower = solve_placed(
        (child_block, 0, prow_count), within, [panel], child_inverse, 0, root_tiles, False
    )
    rights = solve_cols(early, 0, 1)

    swap = [(0, 1), (1, 0)]
    incoming = []

    def send(index, after):
        outgoing = contribution(
            out_tables,
            within,
            child_update,
            out_lower,
            rights,
            *chunks[index],
            after=after,
            flops=0,
        )
        incoming.append(lax.ppermute(outgoing, "half", swap))
        return outgoing

    outgoing = send(0, [])
    middle = fetch(*spans[1], [outgoing])
    rights += solve_cols(early, 1, spans[0][1] - 1, [middle[0]], 1)
    outgoing = send(1, [outgoing])
    kept_lower = solve_placed(
        (child_block, root_tiles, prow_count), within, [panel], child_inverse, 0, root_tiles, False, [outgoing]
    )
    kept = contribution(
        kept_tables, within, child_update, kept_lower, rights, 0, 1, root_front
    )
    lead = hold([kept, incoming[0]], [])
    gathered = lax.all_gather(lead, "pcol", axis=0, tiled=True)
    rights += solve_cols(middle, *spans[1])
    late = fetch(*spans[2], [lead])
    outgoing = late[0]
    for index in (2, 3):
        outgoing = send(index, [outgoing])
    if sum(chunks[4]) <= len(rights):
        outgoing = send(4, [outgoing])
    rights += solve_cols(late, *spans[2], after=[outgoing, incoming[1]])
    if len(incoming) < 5:
        outgoing = send(4, [outgoing])
    row_group = (half_index * prow_count + row_index).astype(jnp.int32)
    root_panel, shared = join(
        jnp.stack([keep[0], row_group]),
        gathered,
        half_rows,
        prow_count,
        [rights[-1][0]] + incoming[2:4],
    )
    share = lax.psum_scatter(shared, "prow", scatter_dimension=0, tiled=True)
    outgoing = root_panel
    for index in range(5, len(chunks)):
        outgoing = send(index, [outgoing])
    share = hold([share], [outgoing] + incoming[4:5])
    rows = half_rows // prow_count
    pair = lax.all_gather(share, "half", axis=0)
    pivots = lax.all_gather(pair[0, rows:], "prow", axis=0, tiled=True)
    root_factor, root_inverse = factor_and_inverse(pivots)
    pair = lower_part(pair, rows, incoming[5:6])
    acc = contribution(
        kept_tables,
        within,
        child_update,
        kept_lower,
        rights,
        0,
        col_tiles,
        root_front,
        [pair],
    )
    pair = lax.all_gather(pair, "prow", axis=0)
    block = next(b for b in (512, 256) if half_rows % b == 0)
    lower = solve(root_panel, root_inverse, block)
    leading = lax.dynamic_slice_in_dim(root_factor, jnp.minimum(row_group, 1) * TB, TB, 0)
    lower = lower.at[:TB].set(jnp.where(row_group < 2, leading, lower[:TB]))
    root_cols = solve_groups(pair, root_inverse, rows)

    place = jnp.stack(
        [row_group, jnp.asarray(2 * prow_count, jnp.int32), col_index.astype(jnp.int32)]
    )
    early_count = min(6, len(chunks) - 1)
    acc = finish(place, acc, incoming[:early_count], lower, root_cols, pcol_count)
    for (first, count), arrived in list(zip(chunks, incoming))[early_count:]:
        acc = add_piece(acc, arrived, first, count)
    return (lower, acc)


def solution(mesh):
    placed = (
        P("half", None, None),
        P("half", "prow", None),
        P("half", "prow", "pcol"),
        P(("half", "prow"), "pcol"),
        P(),
    )
    return jax.shard_map(
        local,
        mesh=mesh,
        in_specs=placed,
        out_specs=(P(("half", "prow"), None), P(("half", "prow"), "pcol")),
        check_vma=False,
    )
```
